32 devices in a mesh: rep: 2 (over y), fsdp: 8 (over z, x), tp: 2 (over core).
Axes of the slice: x: 2, y: 2, z: 4, core: 2. Of those that a mesh axis runs over, the one named last changes fastest.
Arguments:
- attn_global: float32 [24, 1024, 1024], P('rep', 'fsdp', 'tp'), may hold values from -6 to 6
- attn_momentum: float32 [24, 1024, 1024], P('rep', 'fsdp', 'tp'), may hold values from -6 to 6
- attn_inner: bfloat16 [2, 24, 1024, 1024], P('rep', None, 'fsdp', 'tp'), may hold values from -6 to 6
- norm_global: float32 [4, 1024], P('rep', 'tp'), may hold values from 0.5 to 1.5
- norm_momentum: float32 [4, 1024], P('rep', 'tp'), may hold values from -4 to 4
- norm_inner: bfloat16 [2, 4, 1024], P('rep', None, 'tp'), may hold values from 0.5 to 1.5
- emb_global: float32 [8, 2, 2008, 1024], P('fsdp', 'rep', None, 'tp'), may hold values from -6 to 6
- emb_momentum: float32 [8, 2, 2008, 1024], P('fsdp', 'rep', None, 'tp'), may hold values from -6 to 6
- emb_inner: bfloat16 [2, 32128, 1024], P('rep', 'fsdp', 'tp'), may hold values from -6 to 6
- basis: float32 [1024, 64], replicated, may hold values from -0.1875 to 0.1875
- touched: int32 [2, 8192], replicated, may hold values from 0 to 32127
Outputs:
- new_attn_global: float32 [24, 1024, 1024], P('rep', 'fsdp', 'tp')
- new_attn_momentum: float32 [24, 1024, 1024], P('rep', 'fsdp', 'tp')
- attn_weights: float32 [24, 1024, 1024], P(None, 'fsdp', 'tp')
- new_norm_global: float32 [4, 1024], P('rep', 'tp')
- new_norm_momentum: float32 [4, 1024], P('rep', 'tp')
- norm_weights: float32 [4, 1024], P(None, 'tp')
- new_emb_global: float32 [8, 2, 2008, 1024], P('fsdp', 'rep', None, 'tp')
- new_emb_momentum: float32 [8, 2, 2008, 1024], P('fsdp', 'rep', None, 'tp')
- emb_weights: float32 [32128, 1024], P('fsdp', 'tp')
The draws below stay inside these ranges and needn't reach their ends.
All inputs are finite; a program needn't handle non-finite values.
Results may differ from the reference program's by a relative error of at most 0.0003.
Values sent between devices are 32-bit elements; how exact they have to be, the bound alone decides.
A program may use at most 128 MiB of HBM per device.

```python
import jax
import jax.numpy as jnp
from jax import lax

D = 1024
VOCAB = 32128
RANK = 64
MATS = 24
NORMS = 4
TOUCHED = 8192
REPS = 2
EMB_BLOCKS = 8
EMB_ROWS = 2008


def touch_ends(drawn, own_key, smallest, high):
    shape = drawn.shape
    index_at = [jax.random.randint(jax.random.fold_in(own_key, axis), (), 0, shape[axis]) for axis in range(len(shape))]
    drawn = drawn.at[tuple(index_at)].set(smallest)
    longest = shape.index(max(shape))
    index_at[longest] = (index_at[longest] + 1) % shape[longest]
    return drawn.at[tuple(index_at)].set(high)


def shard_levels(own_key, dims, split, low, top_value):
    def one(axis_at, parts):
        draws = jax.random.uniform(jax.random.fold_in(jax.random.fold_in(own_key, 6), axis_at), (parts,), jnp.float32, low / len(split), top_value / len(split))
        return jnp.repeat(jnp.exp(draws), dims[axis_at] // parts).reshape((-1,) + (1,) * (len(dims) - axis_at - 1))

    loudness = one(*split[0])
    for cut in split[1:]:
        loudness = loudness * one(*cut)
    return loudness


def bell_draw(rng, extent, scale, reach, split=(), kind=jnp.bfloat16):
    result = jax.random.normal(rng, extent, jnp.float32) * scale
    if len(split) > 0:
        result = shard_levels(rng, extent, split, -0.22, 0.18) * result
    return jnp.clip(result, min=-reach, max=reach).astype(kind)


def setup_inputs(seed: int = 0) -> dict:
    splits = jax.random.split(jax.random.key(seed), 12)
    return {
        "attn_global": bell_draw(splits[0], (MATS, D, D), 1.0, 6.0, ((0, 2), (1, 8), (2, 2)), jnp.float32),
        "attn_momentum": bell_draw(splits[1], (MATS, D, D), 1.0, 6.0, ((0, 2), (1, 8), (2, 2)), jnp.float32),
        "attn_inner": bell_draw(splits[2], (REPS, MATS, D, D), 1.0, 6.0, ((0, 2), (2, 8), (3, 2))),
        "norm_global": jnp.clip(1.0 + 0.1 * jax.random.normal(splits[3], (NORMS, D), jnp.float32), 0.5, 1.5),
        "norm_momentum": bell_draw(splits[4], (NORMS, D), 0.3, 4.0, ((0, 2), (1, 2)), jnp.float32),
        "norm_inner": jnp.clip(1.0 + 0.1 * jax.random.normal(splits[5], (REPS, NORMS, D), jnp.float32), 0.5, 1.5).astype(jnp.bfloat16),
        "emb_global": bell_draw(splits[6], (EMB_BLOCKS, REPS, EMB_ROWS, D), 1.0, 6.0, ((0, 8), (1, 2), (3, 2)), jnp.float32),
        "emb_momentum": bell_draw(splits[7], (EMB_BLOCKS, REPS, EMB_ROWS, D), 1.0, 6.0, ((0, 8), (1, 2), (3, 2)), jnp.float32),
        "emb_inner": bell_draw(splits[8], (REPS, VOCAB, D), 1.0, 6.0, ((0, 2), (1, 8), (2, 2))),
        "basis": bell_draw(splits[9], (D, RANK), D ** -0.5, 0.1875, (), jnp.float32),
        "touched": touch_ends(jax.random.randint(splits[10], (REPS, TOUCHED), 0, VOCAB), jax.random.fold_in(splits[10], 1), 0, VOCAB - 1).astype(jnp.int32),
    }


OUTER_RATE = 0.7
MOMENTUM = 0.9


def nesterov(global_part, momentum_part, outer_grad):
    fresh_momentum = MOMENTUM * momentum_part + outer_grad
    fresh_global = global_part - OUTER_RATE * (outer_grad + MOMENTUM * fresh_momentum)
    return fresh_global, fresh_momentum


def reference(attn_global, attn_momentum, attn_inner, norm_global, norm_momentum, norm_inner, emb_global, emb_momentum, emb_inner, basis, touched):
    groups = REPS * 1.0
    attn_grad = attn_global - jnp.sum(attn_inner.astype(jnp.float32), axis=0) / groups
    new_attn_global, new_attn_momentum = nesterov(attn_global, attn_momentum, attn_grad)
    attn_weights = new_attn_global
    norm_grad = norm_global - jnp.sum(norm_inner.astype(jnp.float32), axis=0) / groups
    new_norm_global, new_norm_momentum = nesterov(norm_global, norm_momentum, norm_grad)
    norm_weights = new_norm_global
    emb_flat = emb_global.reshape(VOCAB, D)
    momentum_flat = emb_momentum.reshape(VOCAB, D)
    group_rows = jnp.broadcast_to(jnp.arange(REPS, dtype=jnp.int32)[:, None], touched.shape)
    touched_masks = jnp.zeros((REPS, VOCAB), jnp.float32).at[group_rows, touched].set(1.0)
    global_coeff = jnp.dot(emb_flat, basis, precision=lax.Precision.HIGHEST, preferred_element_type=jnp.float32)
    coeff_sum = jnp.zeros((VOCAB, RANK), jnp.float32)
    for group in range(REPS):
        inner_coeff = jnp.dot(emb_inner[group].astype(jnp.float32), basis, precision=lax.Precision.HIGHEST, preferred_element_type=jnp.float32)
        coeff_sum = coeff_sum + touched_masks[group][:, None] * (global_coeff - inner_coeff)
    emb_grad = jnp.dot(coeff_sum, basis.T, precision=lax.Precision.HIGHEST, preferred_element_type=jnp.float32) / groups
    flat_global, flat_momentum = nesterov(emb_flat, momentum_flat, emb_grad)
    new_emb_global = flat_global.reshape(EMB_BLOCKS, REPS, EMB_ROWS, D)
    new_emb_momentum = flat_momentum.reshape(EMB_BLOCKS, REPS, EMB_ROWS, D)
    emb_weights = flat_global
    return (new_attn_global, new_attn_momentum, attn_weights, new_norm_global, new_norm_momentum, norm_weights, new_emb_global, new_emb_momentum, emb_weights)
```

```python
import jax
import jax.numpy as jnp
from jax import lax
from jax.sharding import PartitionSpec as P

OUTER_RATE = 0.7
MOMENTUM = 0.9
SWAP = ((0, 1), (1, 0))
ATTN_CHUNKS = 2
EMB_CHUNKS = 4
LOW = 256


def nesterov(global_part, momentum_part, outer_grad):
    fresh_momentum = MOMENTUM * momentum_part + outer_grad
    fresh_global = global_part - OUTER_RATE * (outer_grad + MOMENTUM * fresh_momentum)
    return (fresh_global, fresh_momentum)


def cuts(total, parts, unit):
    units = -(-total // unit)
    bounds = [min(total, unit * (units * i // parts)) for i in range(parts + 1)]
    return [(a, b) for a, b in zip(bounds[:-1], bounds[1:]) if b > a]


def swap(x, axis):
    return lax.ppermute(x, axis, SWAP)


def row_masks(touched, row_start, block_rows):
    high_count = -(-block_rows // LOW)
    local = touched - row_start
    high = jnp.floor_divide(local, LOW)
    low = local - high * LOW
    high_hot = (high[:, None, :] == jnp.arange(high_count, dtype=jnp.int32)[None, :, None]).astype(jnp.bfloat16)
    low_hot = (low[:, None, :] == jnp.arange(LOW, dtype=jnp.int32)[None, :, None]).astype(jnp.bfloat16)
    times = jnp.einsum("rht,rlt->rhl", high_hot, low_hot, preferred_element_type=jnp.float32)
    masks = (times > 0.5).astype(jnp.float32)
    return masks.reshape(touched.shape[0], high_count * LOW)[:, :block_rows]


def coeff_of(rows, basis_half):
    return lax.dot_general(
        basis_half,
        rows,
        (((0,), (1,)), ((), ())),
        precision=lax.Precision.HIGHEST,
        preferred_element_type=jnp.float32,
    )


def per_device(
    attn_global,
    attn_momentum,
    attn_inner,
    norm_global,
    norm_momentum,
    norm_inner,
    emb_global,
    emb_momentum,
    emb_inner,
    basis,
    touched,
):
    groups = lax.axis_size("rep") * 1.0
    rep_index = lax.axis_index("rep")
    tp_index = lax.axis_index("tp")
    other = 1 - rep_index
    attn_owned = attn_global.shape[0]
    norm_owned = norm_global.shape[0]
    block_rows = emb_inner.shape[1]
    half_rows = emb_global.shape[2]
    half_width = emb_global.shape[3]
    rank = basis.shape[1]

    attn_cuts = cuts(attn_owned, ATTN_CHUNKS, 1)
    arrived = []
    for a, b in attn_cuts:
        part = lax.dynamic_slice_in_dim(attn_inner[0], other * attn_owned + a, b - a, 0)
        arrived.append(swap(part.astype(jnp.float32) / groups, "rep"))
    norm_part = lax.dynamic_slice_in_dim(norm_inner[0], other * norm_owned, norm_owned, 0)
    norm_arrived = swap(norm_part.astype(jnp.float32) / groups, "rep")

    half_start = rep_index * half_rows
    other_start = other * half_rows
    masks = row_masks(touched, lax.axis_index("fsdp") * block_rows, block_rows)
    counts = jnp.sum(masks, axis=0)
    own_mask = lax.dynamic_index_in_dim(masks, rep_index, 0, keepdims=False)
    half_counts = lax.dynamic_slice_in_dim(counts, half_start, half_rows, 0)
    basis_half = lax.dynamic_slice_in_dim(basis, tp_index * half_width, half_width, 0)
    own_rows = emb_global[0, 0]
    own_momentum = emb_momentum[0, 0]
    global_coeff = half_counts[None, :] * coeff_of(own_rows, basis_half)
    inner_coeff = own_mask[None, :] * coeff_of(emb_inner[0].astype(jnp.float32), basis_half)
    own_term = global_coeff - lax.dynamic_slice_in_dim(inner_coeff, half_start, half_rows, 1)
    other_term = -lax.dynamic_slice_in_dim(inner_coeff, other_start, half_rows, 1)
    terms = jnp.stack((own_term, other_term))
    half_rank = rank // 2
    kept = lax.dynamic_slice_in_dim(terms, tp_index * half_rank, half_rank, 1)
    given = lax.dynamic_slice_in_dim(terms, (1 - tp_index) * half_rank, half_rank, 1)
    summed = kept + swap(given, "tp")
    coeff_mine = summed[0] + swap(summed[1], "rep")
    coeff_theirs = swap(coeff_mine, "tp")
    first = tp_index == 0
    coeff_sum = jnp.concatenate(
        (
            jnp.where(first, coeff_mine, coeff_theirs),
            jnp.where(first, coeff_theirs, coeff_mine),
        ),
        axis=0,
    )
    emb_grad = (
        lax.dot_general(
            coeff_sum,
            basis_half,
            (((0,), (1,)), ((), ())),
            precision=lax.Precision.HIGHEST,
            preferred_element_type=jnp.float32,
        )
        / groups
    )
    fresh_rows, fresh_momentum = nesterov(own_rows, own_momentum, emb_grad)

    fresh_global = []
    fresh_attn_momentum = []
    returned = []
    for (a, b), got in zip(attn_cuts, arrived):
        part = lax.dynamic_slice_in_dim(attn_inner[0], rep_index * attn_owned + a, b - a, 0)
        mean = part.astype(jnp.float32) / groups + got
        now, moved = nesterov(attn_global[a:b], attn_momentum[a:b], attn_global[a:b] - mean)
        fresh_global.append(now)
        fresh_attn_momentum.append(moved)
        returned.append(swap(now, "rep"))
    new_attn_global = jnp.concatenate(fresh_global, axis=0)
    new_attn_momentum = jnp.concatenate(fresh_attn_momentum, axis=0)
    attn_weights = jnp.zeros((2 * attn_owned,) + attn_global.shape[1:], jnp.float32)
    attn_weights = lax.dynamic_update_slice_in_dim(attn_weights, new_attn_global, rep_index * attn_owned, 0)
    for (a, b), got in zip(attn_cuts, returned):
        attn_weights = lax.dynamic_update_slice_in_dim(attn_weights, got, other * attn_owned + a, 0)

    norm_own = lax.dynamic_slice_in_dim(norm_inner[0], rep_index * norm_owned, norm_owned, 0)
    norm_mean = norm_own.astype(jnp.float32) / groups + norm_arrived
    new_norm_global, new_norm_momentum = nesterov(norm_global, norm_momentum, norm_global - norm_mean)
    norm_weights = jnp.zeros((2 * norm_owned,) + norm_global.shape[1:], jnp.float32)
    norm_weights = lax.dynamic_update_slice_in_dim(norm_weights, new_norm_global, rep_index * norm_owned, 0)
    norm_weights = lax.dynamic_update_slice_in_dim(
        norm_weights, swap(new_norm_global, "rep"), other * norm_owned, 0
    )

    emb_weights = jnp.zeros((block_rows, half_width), jnp.float32)
    emb_weights = lax.dynamic_update_slice_in_dim(emb_weights, fresh_rows, half_start, 0)
    for a, b in cuts(half_rows, EMB_CHUNKS, 8):
        got = swap(fresh_rows[a:b], "rep")
        emb_weights = lax.dynamic_update_slice_in_dim(emb_weights, got, other_start + a, 0)

    return (
        new_attn_global,
        new_attn_momentum,
        attn_weights,
        new_norm_global,
        new_norm_momentum,
        norm_weights,
        fresh_rows.reshape(emb_global.shape),
        fresh_momentum.reshape(emb_momentum.shape),
        emb_weights,
    )


def solution(mesh):
    placed = (
        P("rep", "fsdp", "tp"),
        P("rep", "fsdp", "tp"),
        P("rep", None, "fsdp", "tp"),
        P("rep", "tp"),
        P("rep", "tp"),
        P("rep", None, "tp"),
        P("fsdp", "rep", None, "tp"),
        P("fsdp", "rep", None, "tp"),
        P("rep", "fsdp", "tp"),
        P(),
        P(),
    )
    return jax.shard_map(
        per_device,
        mesh=mesh,
        in_specs=placed,
        out_specs=(
            P("rep", "fsdp", "tp"),
            P("rep", "fsdp", "tp"),
            P(None, "fsdp", "tp"),
            P("rep", "tp"),
            P("rep", "tp"),
            P(None, "tp"),
            P("fsdp", "rep", None, "tp"),
            P("fsdp", "rep", None, "tp"),
            P("fsdp", "tp"),
        ),
        check_vma=False,
    )
```

```python
import jax
import jax.numpy as jnp
from jax import lax
from jax.sharding import PartitionSpec as P

OUTER_RATE = 0.7
MOMENTUM = 0.9
SWAP = ((0, 1), (1, 0))
EMB_CUTS = (0, 3, 6, 9, 12)
TWELFTHS = 12
LOW = 256


def nesterov(global_part, momentum_part, outer_grad):
    fresh_momentum = MOMENTUM * momentum_part + outer_grad
    fresh_global = global_part - OUTER_RATE * (outer_grad + MOMENTUM * fresh_momentum)
    return (fresh_global, fresh_momentum)


def cuts(total, marks, unit):
    units = -(-total // unit)
    bounds = [min(total, unit * (units * mark // TWELFTHS)) for mark in marks]
    return [(a, b) for a, b in zip(bounds[:-1], bounds[1:]) if b > a]


def swap(x, axis):
    return lax.ppermute(x, axis, SWAP)


def after(x, earlier):
    return lax.optimization_barrier((x, earlier))[0]


def placed(own, rep_index):
    halves = jnp.zeros((2,) + own.shape, jnp.float32)
    return lax.dynamic_update_slice(halves, own[None], (rep_index,) + (0,) * own.ndim)


def put(halves, piece, at, rep_index):
    return lax.dynamic_update_slice(halves, piece[None], (1 - rep_index, at) + (0,) * (piece.ndim - 1))


def row_masks(touched, row_start, block_rows):
    high_count = -(-block_rows // LOW)
    local = touched - row_start
    high = jnp.floor_divide(local, LOW)
    low = local - high * LOW
    high_hot = (high[:, None, :] == jnp.arange(high_count, dtype=jnp.int32)[None, :, None]).astype(jnp.bfloat16)
    low_hot = (low[:, None, :] == jnp.arange(LOW, dtype=jnp.int32)[None, :, None]).astype(jnp.bfloat16)
    times = jnp.einsum("rht,rlt->rhl", high_hot, low_hot, preferred_element_type=jnp.float32)
    masks = (times > 0.5).astype(jnp.float32)
    return masks.reshape(touched.shape[0], high_count * LOW)[:, :block_rows]


def coeff_of(rows, basis_half):
    return lax.dot_general(
        basis_half,
        rows,
        (((0,), (1,)), ((), ())),
        precision=lax.Precision.HIGHEST,
        preferred_element_type=jnp.float32,
    )


def per_device(
    attn_global,
    attn_momentum,
    attn_inner,
    norm_global,
    norm_momentum,
    norm_inner,
    emb_global,
    emb_momentum,
    emb_inner,
    basis,
    touched,
):
    groups = lax.axis_size("rep") * 1.0
    rep_index = lax.axis_index("rep")
    tp_index = lax.axis_index("tp")
    other = 1 - rep_index
    attn_owned = attn_global.shape[0]
    norm_owned = norm_global.shape[0]
    block_rows = emb_inner.shape[1]
    half_rows = emb_global.shape[2]
    half_width = emb_global.shape[3]
    rank = basis.shape[1]

    width = attn_global.shape[2]

    def pack(attn, norm):
        return jnp.concatenate((attn.reshape(-1, width), norm), axis=0)

    def unpack(rows):
        return rows[:-norm_owned].reshape(attn_global.shape), rows[-norm_owned:]

    def mean_part(inner, owned, owner):
        part = lax.dynamic_slice_in_dim(inner[0], owner * owned, owned, 0)
        return part.astype(jnp.float32) / groups

    leaving = pack(mean_part(attn_inner, attn_owned, other), mean_part(norm_inner, norm_owned, other))
    arrived = swap(leaving, "rep")

    touched = after(touched, leaving)
    masks = row_masks(touched, lax.axis_index("fsdp") * block_rows, block_rows)
    masks = masks.reshape(masks.shape[0], 2, half_rows)
    own_mask = lax.dynamic_index_in_dim(masks, rep_index, 0, keepdims=False)
    half_counts = lax.dynamic_index_in_dim(jnp.sum(masks, axis=0), rep_index, 0, keepdims=False)
    mask_kept = lax.dynamic_index_in_dim(own_mask, rep_index, 0, keepdims=False)
    mask_given = lax.dynamic_index_in_dim(own_mask, other, 0, keepdims=False)
    basis_half = lax.dynamic_slice_in_dim(basis, tp_index * half_width, half_width, 0)
    own_rows = emb_global[0, 0]
    own_momentum = emb_momentum[0, 0]
    inner_halves = emb_inner[0].reshape(2, half_rows, half_width)
    inner_kept = lax.dynamic_index_in_dim(inner_halves, rep_index, 0, keepdims=False)
    inner_given = lax.dynamic_index_in_dim(inner_halves, other, 0, keepdims=False)
    half_rank = rank // 2
    terms = jnp.stack(
        (
            half_counts[None, :] * coeff_of(own_rows, basis_half)
            - mask_kept[None, :] * coeff_of(inner_kept.astype(jnp.float32), basis_half),
            -mask_given[None, :] * coeff_of(inner_given.astype(jnp.float32), basis_half),
        )
    )
    kept = lax.dynamic_slice_in_dim(terms, tp_index * half_rank, half_rank, 1)
    given = lax.dynamic_slice_in_dim(terms, (1 - tp_index) * half_rank, half_rank, 1)
    summed = kept + swap(given, "tp")
    coeff_arrived = swap(summed[1], "rep")

    attn_arrived, norm_arrived = unpack(after(arrived, summed))
    attn_mean = mean_part(attn_inner, attn_owned, rep_index) + attn_arrived
    norm_mean = mean_part(norm_inner, norm_owned, rep_index) + norm_arrived
    new_attn_global, new_attn_momentum = nesterov(attn_global, attn_momentum, attn_global - attn_mean)
    new_norm_global, new_norm_momentum = nesterov(norm_global, norm_momentum, norm_global - norm_mean)
    back = pack(new_attn_global, new_norm_global)
    returned = swap(back, "rep")

    coeff_mine = summed[0] + after(coeff_arrived, back)
    coeff_theirs = swap(coeff_mine, "tp")
    first = tp_index == 0
    coeff_sum = jnp.concatenate(
        (
            jnp.where(first, coeff_mine, coeff_theirs),
            jnp.where(first, coeff_theirs, coeff_mine),
        ),
        axis=0,
    )
    emb_grad = (
        lax.dot_general(
            coeff_sum,
            basis_half,
            (((0,), (1,)), ((), ())),
            precision=lax.Precision.HIGHEST,
            preferred_element_type=jnp.float32,
        )
        / groups
    )
    fresh_rows, fresh_momentum = nesterov(own_rows, own_momentum, emb_grad)
    emb_cuts = cuts(half_rows, EMB_CUTS, 8)
    emb_returned = [swap(fresh_rows[a:b], "rep") for a, b in emb_cuts]

    attn_returned, norm_returned = unpack(returned)
    attn_weights = put(placed(new_attn_global, rep_index), attn_returned, 0, rep_index)
    norm_weights = put(placed(new_norm_global, rep_index), norm_returned, 0, rep_index)
    emb_weights = placed(fresh_rows, rep_index)
    for i, ((a, _), got) in enumerate(zip(emb_cuts, emb_returned)):
        if i >= 1:
            got = after(got, (attn_weights, norm_weights))
        emb_weights = put(emb_weights, got, a, rep_index)
    attn_weights, norm_weights, emb_weights = [
        halves.reshape((-1,) + halves.shape[2:]) for halves in (attn_weights, norm_weights, emb_weights)
    ]

    return (
        new_attn_global,
        new_attn_momentum,
        attn_weights,
        new_norm_global,
        new_norm_momentum,
        norm_weights,
        fresh_rows.reshape(emb_global.shape),
        fresh_momentum.reshape(emb_momentum.shape),
        emb_weights,
    )


def solution(mesh):
    placed = (
        P("rep", "fsdp", "tp"),
        P("rep", "fsdp", "tp"),
        P("rep", None, "fsdp", "tp"),
        P("rep", "tp"),
        P("rep", "tp"),
        P("rep", None, "tp"),
        P("fsdp", "rep", None, "tp"),
        P("fsdp", "rep", None, "tp"),
        P("rep", "fsdp", "tp"),
        P(),
        P(),
    )
    return jax.shard_map(
        per_device,
        mesh=mesh,
        in_specs=placed,
        out_specs=(
            P("rep", "fsdp", "tp"),
            P("rep", "fsdp", "tp"),
            P(None, "fsdp", "tp"),
            P("rep", "tp"),
            P("rep", "tp"),
            P(None, "tp"),
            P("fsdp", "rep", None, "tp"),
            P("fsdp", "rep", None, "tp"),
            P("fsdp", "tp"),
        ),
        check_vma=False,
    )
```

```python
import jax
import jax.numpy as jnp
from jax import lax
from jax.sharding import PartitionSpec as P

OUTER_RATE = 0.7
MOMENTUM = 0.9
SWAP = ((0, 1), (1, 0))
EMB_CUTS = (0, 4, 8, 10, 11, 12)
TWELFTHS = 12
LOW = 256


def nesterov(global_part, momentum_part, outer_grad):
    fresh_momentum = MOMENTUM * momentum_part + outer_grad
    fresh_global = global_part - OUTER_RATE * (outer_grad + MOMENTUM * fresh_momentum)
    return (fresh_global, fresh_momentum)


def cuts(total, marks, unit):
    units = -(-total // unit)
    bounds = [min(total, unit * (units * mark // TWELFTHS)) for mark in marks]
    return [(a, b) for a, b in zip(bounds[:-1], bounds[1:]) if b > a]


def swap(x, axis):
    return lax.ppermute(x, axis, SWAP)


def after(x, earlier):
    return lax.optimization_barrier((x, earlier))[0]


def placed(own, rep_index):
    halves = jnp.zeros((2,) + own.shape, jnp.float32)
    return lax.dynamic_update_slice(halves, own[None], (rep_index,) + (0,) * own.ndim)


def put(halves, piece, at, rep_index):
    return lax.dynamic_update_slice(halves, piece[None], (1 - rep_index, at) + (0,) * (piece.ndim - 1))


def row_masks(touched, row_start, block_rows):
    high_count = -(-block_rows // LOW)
    local = touched - row_start
    high = jnp.floor_divide(local, LOW)
    low = local - high * LOW
    high_hot = (high[:, None, :] == jnp.arange(high_count, dtype=jnp.int32)[None, :, None]).astype(jnp.bfloat16)
    low_hot = (low[:, None, :] == jnp.arange(LOW, dtype=jnp.int32)[None, :, None]).astype(jnp.bfloat16)
    times = jnp.einsum("rht,rlt->rhl", high_hot, low_hot, preferred_element_type=jnp.float32)
    masks = (times > 0.5).astype(jnp.float32)
    return masks.reshape(touched.shape[0], high_count * LOW)[:, :block_rows]


def coeff_of(rows, basis_half):
    return lax.dot_general(
        basis_half,
        rows,
        (((0,), (1,)), ((), ())),
        precision=lax.Precision.HIGHEST,
        preferred_element_type=jnp.float32,
    )


def per_device(
    attn_global,
    attn_momentum,
    attn_inner,
    norm_global,
    norm_momentum,
    norm_inner,
    emb_global,
    emb_momentum,
    emb_inner,
    basis,
    touched,
):
    groups = lax.axis_size("rep") * 1.0
    rep_index = lax.axis_index("rep")
    tp_index = lax.axis_index("tp")
    other = 1 - rep_index
    attn_owned = attn_global.shape[0]
    norm_owned = norm_global.shape[0]
    block_rows = emb_inner.shape[1]
    half_rows = emb_global.shape[2]
    half_width = emb_global.shape[3]
    rank = basis.shape[1]

    def mean_part(owner):
        part = lax.dynamic_slice_in_dim(attn_inner[0], owner * attn_owned, attn_owned, 0)
        return part.astype(jnp.float32) / groups

    leaving = mean_part(other)
    arrived = swap(leaving, "rep")

    touched = after(touched, leaving)
    masks = row_masks(touched, lax.axis_index("fsdp") * block_rows, block_rows)
    masks = masks.reshape(masks.shape[0], 2, half_rows)
    own_mask = lax.dynamic_index_in_dim(masks, rep_index, 0, keepdims=False)
    half_counts = lax.dynamic_index_in_dim(jnp.sum(masks, axis=0), rep_index, 0, keepdims=False)
    mask_kept = lax.dynamic_index_in_dim(own_mask, rep_index, 0, keepdims=False)
    mask_given = lax.dynamic_index_in_dim(own_mask, other, 0, keepdims=False)
    basis_half = lax.dynamic_slice_in_dim(basis, tp_index * half_width, half_width, 0)
    own_rows = emb_global[0, 0]
    own_momentum = emb_momentum[0, 0]
    inner_halves = emb_inner[0].reshape(2, half_rows, half_width)
    inner_kept = lax.dynamic_index_in_dim(inner_halves, rep_index, 0, keepdims=False)
    inner_given = lax.dynamic_index_in_dim(inner_halves, other, 0, keepdims=False)
    half_rank = rank // 2
    terms = jnp.stack(
        (
            half_counts[None, :] * coeff_of(own_rows, basis_half)
            - mask_kept[None, :] * coeff_of(inner_kept.astype(jnp.float32), basis_half),
            -mask_given[None, :] * coeff_of(inner_given.astype(jnp.float32), basis_half),
        )
    )
    kept = lax.dynamic_slice_in_dim(terms, tp_index * half_rank, half_rank, 1)
    given = lax.dynamic_slice_in_dim(terms, (1 - tp_index) * half_rank, half_rank, 1)
    summed = kept + swap(given, "tp")

    norm_sent = jnp.concatenate((norm_inner[0].astype(jnp.float32) / groups, norm_global, norm_momentum), axis=0)
    norm_lines = -(-norm_sent.size // half_rows)
    norm_flat = jnp.pad(norm_sent.reshape(-1), (0, norm_lines * half_rows - norm_sent.size))
    packed = jnp.concatenate((summed[1], norm_flat.reshape(norm_lines, half_rows)), axis=0)
    packed_arrived = swap(packed, "rep")

    attn_mean = mean_part(rep_index) + after(arrived, packed)
    new_attn_global, _ = nesterov(attn_global, attn_momentum, attn_global - attn_mean)
    returned = swap(new_attn_global, "rep")

    packed_arrived = after(packed_arrived, new_attn_global)
    coeff_arrived = packed_arrived[:half_rank]
    norm_got = packed_arrived[half_rank:].reshape(-1)[: norm_sent.size].reshape(norm_sent.shape)

    coeff_mine = summed[0] + coeff_arrived
    coeff_theirs = swap(coeff_mine, "tp")
    first = tp_index == 0
    coeff_sum = jnp.concatenate(
        (
            jnp.where(first, coeff_mine, coeff_theirs),
            jnp.where(first, coeff_theirs, coeff_mine),
        ),
        axis=0,
    )
    emb_grad = (
        lax.dot_general(
            coeff_sum,
            basis_half,
            (((0,), (1,)), ((), ())),
            precision=lax.Precision.HIGHEST,
            preferred_element_type=jnp.float32,
        )
        / groups
    )
    fresh_rows, fresh_momentum = nesterov(own_rows, own_momentum, emb_grad)
    emb_cuts = cuts(half_rows, EMB_CUTS, 8)
    emb_weights = placed(fresh_rows, rep_index)
    emb_returned = []
    for i, (a, b) in enumerate(emb_cuts):
        piece = fresh_rows[a:b]
        if i >= 2:
            emb_weights = put(emb_weights, emb_returned[i - 2], emb_cuts[i - 2][0], rep_index)
            piece = after(piece, emb_weights)
        emb_returned.append(swap(piece, "rep"))

    late, late_own = after((arrived, new_attn_global), fresh_rows)
    late_mean = mean_part(rep_index) + late
    _, new_attn_momentum = nesterov(attn_global, attn_momentum, attn_global - late_mean)
    attn_weights = put(placed(late_own, rep_index), returned, 0, rep_index)
    inner_rows = norm_inner.shape[1]
    norm_total = norm_sent[:inner_rows] + norm_got[:inner_rows]
    norm_mean = lax.dynamic_slice_in_dim(norm_total, rep_index * norm_owned, norm_owned, 0)
    new_norm_global, new_norm_momentum = nesterov(norm_global, norm_momentum, norm_global - norm_mean)
    norm_theirs = norm_got[inner_rows : inner_rows + norm_owned]
    norm_mean = lax.dynamic_slice_in_dim(norm_total, other * norm_owned, norm_owned, 0)
    norm_returned, _ = nesterov(norm_theirs, norm_got[inner_rows + norm_owned :], norm_theirs - norm_mean)
    norm_weights = put(placed(new_norm_global, rep_index), norm_returned, 0, rep_index)
    done = (attn_weights, norm_weights, new_attn_momentum, new_norm_momentum)
    for (a, _), got in list(zip(emb_cuts, emb_returned))[-2:]:
        emb_weights = put(emb_weights, after(got, done), a, rep_index)
    attn_weights, norm_weights, emb_weights = [
        halves.reshape((-1,) + halves.shape[2:]) for halves in (attn_weights, norm_weights, emb_weights)
    ]

    return (
        new_attn_global,
        new_attn_momentum,
        attn_weights,
        new_norm_global,
        new_norm_momentum,
        norm_weights,
        fresh_rows.reshape(emb_global.shape),
        fresh_momentum.reshape(emb_momentum.shape),
        emb_weights,
    )


def solution(mesh):
    placed = (
        P("rep", "fsdp", "tp"),
        P("rep", "fsdp", "tp"),
        P("rep", None, "fsdp", "tp"),
        P("rep", "tp"),
        P("rep", "tp"),
        P("rep", None, "tp"),
        P("fsdp", "rep", None, "tp"),
        P("fsdp", "rep", None, "tp"),
        P("rep", "fsdp", "tp"),
        P(),
        P(),
    )
    return jax.shard_map(
        per_device,
        mesh=mesh,
        in_specs=placed,
        out_specs=(
            P("rep", "fsdp", "tp"),
            P("rep", "fsdp", "tp"),
            P(None, "fsdp", "tp"),
            P("rep", "tp"),
            P("rep", "tp"),
            P(None, "tp"),
            P("fsdp", "rep", None, "tp"),
            P("fsdp", "rep", None, "tp"),
            P("fsdp", "tp"),
        ),
        check_vma=False,
    )
```
